32 devices in a mesh: blk: 8 (over z, x), rep: 4 (over y, core).
Axes of the slice: x: 2, y: 2, z: 4, core: 2. Of those that a mesh axis runs over, the one named last changes fastest.
Arguments:
- orbitals: bfloat16 [32, 32, 48, 128], P('blk'), may hold values from -6 to 6
- skew: int32 [4], P('rep'), may hold values from 0 to 7
Outputs:
- exchange_fields: float32 [32, 32, 48, 128], P('blk', 'rep')
The draws below stay inside these ranges and needn't reach their ends.
All inputs are finite; a program needn't handle non-finite values.
Results may differ from the reference program's by a relative error of at most 0.0041.
Values may be sent and summed in bfloat16 or wider, within the bound.
A program may use at most 64 MiB of HBM per device.

```python
import math
import jax
import jax.numpy as jnp
from jax import lax

NX = 32
NY = 48
NZ = 128
ORB_DEV = 4
HOPS = 4
ORBITALS = 32
N_BLK = 8
N_REP = 4


def plant(drawn, stream_key, least, high):
    spot = [jax.random.randint(jax.random.fold_in(stream_key, axis), (), 0, length) for axis, length in enumerate(drawn.shape)]
    longest = drawn.shape.index(max(drawn.shape))
    beside = spot[:longest] + [(spot[longest] + 1) % drawn.shape[longest]] + spot[longest + 1:]
    return drawn.at[tuple(spot)].set(least).at[tuple(beside)].set(high)


def block_scale(rng, extent, pieces, low, high):
    def one(axis_at, shards_of):
        steps = jax.random.uniform(jax.random.fold_in(jax.random.fold_in(rng, 6), axis_at), (shards_of,), jnp.float32, low / len(pieces), high / len(pieces))
        return jnp.repeat(jnp.exp(steps), extent[axis_at] // shards_of).reshape((-1,) + (1,) * (len(extent) - axis_at - 1))

    level = one(*pieces[0])
    for cut in pieces[1:]:
        level = level * one(*cut)
    return level


def noise(key, extent, width, bound, pieces=(), kind=jnp.bfloat16):
    values = jax.random.normal(key, extent, jnp.float32) * width
    if len(pieces) > 0:
        values = block_scale(key, extent, pieces, -0.22, 0.18) * values
    return jnp.clip(values, min=-bound, max=bound).astype(kind)


def setup_inputs(seed: int = 0) -> dict:
    arg_keys = jax.random.split(jax.random.key(seed), 3)
    return {
        "orbitals": noise(arg_keys[0], (ORBITALS, NX, NY, NZ), 1.0, 6.0, ((0, 8),)),
        "skew": plant(jax.random.randint(arg_keys[1], (N_REP,), 0, N_BLK), jax.random.fold_in(arg_keys[1], 1), 0, N_BLK - 1).astype(jnp.int32),
    }


def cas_table(length):
    indices = jnp.arange(length, dtype=jnp.int32)
    products = (indices[:, None] * indices[None, :]) % length
    angles = (2.0 * math.pi / length) * products.astype(jnp.float32)
    return (jnp.cos(angles) + jnp.sin(angles)).astype(jnp.bfloat16)


def frequency_squares(length):
    indices = jnp.arange(length, dtype=jnp.int32)
    signed = jnp.where(indices > length // 2, indices - length, indices)
    wave = (2.0 * math.pi / length) * signed.astype(jnp.float32)
    return wave * wave


def kernel_table():
    squares = frequency_squares(NX)[:, None, None] + frequency_squares(NY)[None, :, None] + frequency_squares(NZ)[None, None, :]
    safe_sq = jnp.where(squares > 0, squares, 1.0)
    kernel = jnp.where(squares > 0, 4.0 * math.pi * (1.0 - jnp.exp(-squares)) / safe_sq, 4.0 * math.pi)
    return kernel / (NX * NY * NZ)


def transform(field, table_x, table_y, table_z):
    first = jnp.einsum('oxyz,zk->oxyk', field.astype(jnp.float32), table_z.astype(jnp.float32)).astype(jnp.bfloat16)
    second = jnp.einsum('oxyz,yk->oxkz', first.astype(jnp.float32), table_y.astype(jnp.float32)).astype(jnp.bfloat16)
    return jnp.einsum('oxyz,xk->okyz', second.astype(jnp.float32), table_x.astype(jnp.float32))


def pair_field(residents, visitor, table_x, table_y, table_z, kernel):
    density = (residents.astype(jnp.float32) * visitor.astype(jnp.float32)[None]).astype(jnp.bfloat16)
    forward = transform(density, table_x, table_y, table_z).astype(jnp.bfloat16)
    scaled = (kernel[None] * forward.astype(jnp.float32)).astype(jnp.bfloat16)
    potential = transform(scaled, table_x, table_y, table_z)
    return potential * visitor.astype(jnp.float32)[None]


def reference(orbitals, skew):
    table_x = cas_table(NX)
    table_y = cas_table(NY)
    table_z = cas_table(NZ)
    kernel = kernel_table()
    owned = orbitals.reshape(N_BLK, ORB_DEV, NX, NY, NZ)
    combos = jnp.arange(N_REP * HOPS, dtype=jnp.int32)
    pairs = jnp.stack([combos // HOPS, combos % HOPS], axis=1)

    def owner_field(owner):
        residents = lax.dynamic_index_in_dim(owned, owner, 0, keepdims=False)

        def advance(field_sum, pair):
            replica = pair[0]
            hop_index = pair[1]
            source = (owner - skew[replica] - hop_index) % N_BLK
            which = (source * ORB_DEV + replica % ORB_DEV).astype(jnp.int32)
            visitor = lax.dynamic_index_in_dim(orbitals, which, 0, keepdims=False)
            return field_sum + pair_field(residents, visitor, table_x, table_y, table_z, kernel), None

        start = jnp.zeros((ORB_DEV, NX, NY, NZ), jnp.float32)
        field_sum, _ = lax.scan(advance, start, pairs)
        return field_sum

    fields = lax.map(owner_field, jnp.arange(N_BLK, dtype=jnp.int32))
    return fields.reshape(ORBITALS, NX, NY, NZ)
```

```python
import functools
import math

import jax
import jax.numpy as jnp
import ml_dtypes
import numpy as np
from jax import lax
from jax.experimental import pallas as pl
from jax.experimental.pallas import tpu as pltpu
from jax.sharding import PartitionSpec as P

HOPS = 4
GROUP = 8
ROWS = 4
COLS = 2
CORES = 2
MESH = pl.DeviceIdType.MESH


def cas_table(length):
    indices = np.arange(length, dtype=np.int32)
    products = indices[:, None] * indices[None, :] % length
    angles = np.float32(2.0 * math.pi / length) * products.astype(np.float32)
    return (np.cos(angles) + np.sin(angles)).astype(ml_dtypes.bfloat16)


def frequency_squares(length):
    indices = np.arange(length, dtype=np.int32)
    signed = np.where(indices > length // 2, indices - length, indices)
    wave = np.float32(2.0 * math.pi / length) * signed.astype(np.float32)
    return wave * wave


def kernel_table(nx, ny, nz):
    squares = (
        frequency_squares(nx)[:, None, None]
        + frequency_squares(ny)[None, :, None]
        + frequency_squares(nz)[None, None, :]
    )
    safe_sq = np.where(squares > 0, squares, np.float32(1.0))
    kernel = np.where(
        squares > 0,
        np.float32(4.0 * math.pi) * -np.expm1(-squares) / safe_sq,
        np.float32(4.0 * math.pi),
    )
    return (kernel / np.float32(nx * ny * nz)).astype(np.float32)


def shifted_2(value, axis, steps):
    count = lax.axis_size(axis)
    pairs = [(source, (source + steps) % count) for source in range(count)]
    return lax.ppermute(value, axis, pairs)


def transform(field, table_x, table_y, table_z):
    first = jnp.einsum("oxyz,zk->oxyk", field, table_z, preferred_element_type=jnp.float32).astype(
        jnp.bfloat16
    )
    second = jnp.einsum("oxyz,yk->oxkz", first, table_y, preferred_element_type=jnp.float32).astype(
        jnp.bfloat16
    )
    return jnp.einsum("oxyz,xk->okyz", second, table_x, preferred_element_type=jnp.float32)


def pair_field(residents, visitor, tables, kernel):
    density = (residents.astype(jnp.float32) * visitor.astype(jnp.float32)[None]).astype(
        jnp.bfloat16
    )
    forward = transform(density, *tables).astype(jnp.bfloat16)
    scaled = (kernel[None] * forward.astype(jnp.float32)).astype(jnp.bfloat16)
    potential = transform(scaled, *tables)
    return potential * visitor.astype(jnp.float32)[None]


def shift_by(visitor, offset):
    for level in range((lax.axis_size("blk") - 1).bit_length()):
        shifted = shifted_2(visitor, "blk", 1 << level)
        visitor = jnp.where(offset // (1 << level) % 2 == 1, shifted, visitor)
    return visitor


def shift_body(orbitals, skew):
    _, nx, ny, nz = orbitals.shape
    tables = [jnp.asarray(cas_table(n)) for n in (nx, ny, nz)]
    kernel = jnp.asarray(kernel_table(nx, ny, nz))
    replica = lax.axis_index("rep")
    start_orb = lax.dynamic_index_in_dim(orbitals, replica % orbitals.shape[0], 0, keepdims=False)
    field_sum = jnp.zeros(orbitals.shape, jnp.float32)
    visitor = shift_by(start_orb, skew[0])
    for hop_index in range(HOPS):
        if hop_index > 0:
            visitor = shifted_2(visitor, "blk", 1)
        field_sum = field_sum + pair_field(orbitals, visitor, tables, kernel)
    return lax.psum_scatter(field_sum, "rep", scatter_dimension=1, tiled=True)


def fields_kernel(
    n_blk, n_rep, skew_ref, orb, tz_ref, ty_ref, tyt_ref, tx_ref, kern_ref, out_ref, *scratch
):
    n_orb, nx, ny, nz = orb.shape
    chunks = nx // ROWS
    levels = n_blk // COLS
    chips = n_rep // CORES
    per_slab = nx // n_rep // ROWS
    groups = ny // GROUP
    rows = ROWS * ny
    sub = ROWS * GROUP
    others = HOPS // COLS
    halves = n_orb // 2
    columns = scratch[:chunks]
    staged = scratch[chunks : 2 * chunks]
    sides = scratch[2 * chunks : 3 * chunks]
    scratch = scratch[3 * chunks :]
    vis, freq, send_core, recv_core, send_chip, recv_chip = scratch[:6]
    line_send, line_recv, side_send, side_recv, core_send, core_recv, chip_send, chip_recv = scratch[
        6:
    ]

    blk = lax.axis_index("blk")
    rep = lax.axis_index("rep")
    level, col = blk // COLS, blk % COLS
    chip, core = rep // CORES, rep % CORES
    side_blk = level * COLS + (COLS - 1 - col)
    core_rep = chip * CORES + (CORES - 1 - core)
    mine = rep % n_orb
    skew = skew_ref[0]

    def chip_rep(step):
        return (chip + step) % chips * CORES + core

    barrier = pltpu.get_barrier_semaphore()
    pl.semaphore_signal(barrier, inc=1, device_id=(side_blk, rep), device_id_type=MESH)
    pl.semaphore_signal(barrier, inc=1, device_id=(blk, core_rep), device_id_type=MESH)
    for step in range(1, chips):
        pl.semaphore_signal(barrier, inc=1, device_id=(blk, chip_rep(step)), device_id_type=MESH)

    @pl.when(level > 0)
    def _():
        pl.semaphore_signal(barrier, inc=1, device_id=(blk - COLS, rep), device_id_type=MESH)

    @pl.when(level < levels - 1)
    def _():
        pl.semaphore_signal(barrier, inc=1, device_id=(blk + COLS, rep), device_id_type=MESH)

    ends = (level == 0).astype(jnp.int32) + (level == levels - 1).astype(jnp.int32)
    pl.semaphore_wait(barrier, 2 + (chips - 1) + 2 - ends)

    def line_copy(c, hop, up):
        source = level - (hop - 1) if up else level + (hop - 1)
        way = 0 if up else 1
        if hop == 1:
            src = orb.at[mine, pl.ds(c * ROWS, ROWS)]
        else:
            src = columns[c].at[source]
        return pltpu.make_async_remote_copy(
            src_ref=src,
            dst_ref=columns[c].at[source],
            send_sem=line_send.at[c, hop - 1, way],
            recv_sem=line_recv.at[c, hop - 1, way],
            device_id=(blk + COLS if up else blk - COLS, rep),
            device_id_type=MESH,
        )

    def line_sends(c, hop, act):
        @pl.when((level < levels - 1) & (level >= hop - 1))
        def _():
            act(line_copy(c, hop, True))

        @pl.when((level > 0) & (level + hop - 1 <= levels - 1))
        def _():
            act(line_copy(c, hop, False))

    def line_arrivals(c, hop):
        def arrival(source, way):
            return pltpu.make_async_remote_copy(
                src_ref=columns[c].at[source],
                dst_ref=columns[c].at[source],
                send_sem=line_send.at[c, hop - 1, way],
                recv_sem=line_recv.at[c, hop - 1, way],
                device_id=(side_blk, rep),
                device_id_type=MESH,
            )

        @pl.when(level >= hop)
        def _():
            arrival(level - hop, 0).wait_recv()

        @pl.when(level + hop <= levels - 1)
        def _():
            arrival(level + hop, 1).wait_recv()

    def side_copy(c):
        return pltpu.make_async_remote_copy(
            src_ref=staged[c],
            dst_ref=sides[c],
            send_sem=side_send.at[c],
            recv_sem=side_recv.at[c],
            device_id=(side_blk, rep),
            device_id_type=MESH,
        )

    def send_side(c):
        first = (side_blk - skew - col) % COLS
        for j in range(others):
            owner = (side_blk - skew - first - COLS * j) % n_blk
            staged[c][j] = columns[c][owner // COLS]
        side_copy(c).start()

    def forward(c):
        for hop in range(HOPS):
            owner = (blk - skew - hop) % n_blk
            vis[hop, pl.ds(c * ROWS, ROWS)] = jnp.where(
                owner % COLS == col, columns[c][owner // COLS], sides[c][hop // COLS]
            )

        def unit(hop, carry):
            visitor = vis[hop, pl.ds(c * ROWS, ROWS)].reshape(rows, nz)
            for half in range(halves):
                density = jnp.concatenate(
                    [
                        orb[2 * half + k, pl.ds(c * ROWS, ROWS)].reshape(rows, nz) * visitor
                        for k in range(2)
                    ],
                    axis=1,
                )
                first = jnp.dot(density, tz_ref[...], preferred_element_type=jnp.float32)
                second = jnp.dot(
                    ty_ref[...], first.astype(jnp.bfloat16), preferred_element_type=jnp.float32
                )
                freq[hop * halves + half, :, pl.ds(c * sub, sub)] = second.astype(
                    jnp.bfloat16
                ).reshape(groups, sub, 2 * nz)
            return carry

        lax.fori_loop(0, HOPS, unit, 0)

    def middle():
        def unit(step, carry):
            group, hop = step // HOPS, step % HOPS
            factor = kern_ref[group]
            for half in range(halves):
                index = hop * halves + half
                third = jnp.dot(
                    tx_ref[...], freq[index, group], preferred_element_type=jnp.float32
                )
                scaled = jnp.concatenate(
                    [third[:, :nz] * factor, third[:, nz:] * factor], axis=1
                ).astype(jnp.bfloat16)
                back = jnp.dot(tx_ref[...], scaled, preferred_element_type=jnp.float32)
                freq[index, group] = back.astype(jnp.bfloat16)
            return carry

        lax.fori_loop(0, groups * HOPS, unit, 0)

    def backward(c, store):
        def unit(half, carry):
            totals = [None, None]
            for hop in range(HOPS):
                visitor = vis[hop, pl.ds(c * ROWS, ROWS)].reshape(rows, nz).astype(jnp.float32)
                spectrum = freq[
                    hop * halves + half, :, pl.ds(pl.multiple_of(c * sub, sub), sub)
                ].reshape(groups * sub, 2 * nz)
                first = jnp.dot(tyt_ref[...], spectrum, preferred_element_type=jnp.float32)
                potential = jnp.dot(
                    first.astype(jnp.bfloat16), tz_ref[...], preferred_element_type=jnp.float32
                )
                for k in range(2):
                    term = potential[:, k * nz : (k + 1) * nz] * visitor
                    totals[k] = term if hop == 0 else totals[k] + term
            for k in range(2):
                store(2 * half + k, totals[k].reshape(ROWS, ny, nz))
            return carry

        lax.fori_loop(0, halves, unit, 0)

    span = levels - 1
    ahead = 1
    for c in range(ahead):
        line_sends(c, 1, lambda copy: copy.start())
    for c in range(chunks):
        columns[c][level] = orb[mine, pl.ds(c * ROWS, ROWS)]
    for step in range(chunks + span + 1):
        if step + ahead < chunks:
            line_sends(step + ahead, 1, lambda copy: copy.start())
        for hop in range(2, span + 1):
            c = step - (hop - 1)
            if 0 <= c < chunks:
                line_arrivals(c, hop - 1)
                line_sends(c, hop, lambda copy: copy.start())
        c = step - span
        if 0 <= c < chunks:
            line_arrivals(c, span)
            send_side(c)
        c = step - span - 1
        if 0 <= c < chunks:
            side_copy(c).wait_recv()
            forward(c)

    middle()

    def core_copy(k, j):
        return pltpu.make_async_remote_copy(
            src_ref=send_core.at[k, j],
            dst_ref=recv_core.at[k, j],
            send_sem=core_send.at[k, j],
            recv_sem=core_recv.at[k, j],
            device_id=(blk, core_rep),
            device_id_type=MESH,
        )

    def chip_copy(k, j):
        return pltpu.make_async_remote_copy(
            src_ref=send_chip.at[k - 1, j],
            dst_ref=recv_chip.at[k - 1, j],
            send_sem=chip_send.at[k - 1, j],
            recv_sem=chip_recv.at[k - 1, j],
            device_id=(blk, chip_rep(k)),
            device_id_type=MESH,
        )

    for k in list(range(1, chips)) + [0]:
        home = (chip + k) % chips * CORES
        for j in range(per_slab):

            def store_core(orbital, value):
                send_core[k, j, orbital] = value.astype(jnp.bfloat16)

            backward((home + CORES - 1 - core) * per_slab + j, store_core)
            core_copy(k, j).start()
            if k > 0:

                def store_chip(orbital, value):
                    send_chip[k - 1, j, orbital] = value.astype(jnp.bfloat16)

                def store_partial(orbital, value):
                    out_ref[orbital, pl.ds(j * ROWS, ROWS)] = value

                backward((home + core) * per_slab + j, store_partial)
                core_copy(k, j).wait_recv()
                for orbital in range(n_orb):
                    store_chip(
                        orbital,
                        out_ref[orbital, pl.ds(j * ROWS, ROWS)]
                        + recv_core[k, j, orbital].astype(jnp.float32),
                    )
                chip_copy(k, j).start()
    for j in range(per_slab):

        def store_out(orbital, value):
            out_ref[orbital, pl.ds(j * ROWS, ROWS)] = value

        backward(rep * per_slab + j, store_out)
    for j in range(per_slab):
        core_copy(0, j).wait_recv()
        for k in range(1, chips):
            chip_copy(k, j).wait_recv()
        for orbital in range(n_orb):
            total = out_ref[orbital, pl.ds(j * ROWS, ROWS)]
            total = total + recv_core[0, j, orbital].astype(jnp.float32)
            for k in range(1, chips):
                total = total + recv_chip[k - 1, j, orbital].astype(jnp.float32)
            out_ref[orbital, pl.ds(j * ROWS, ROWS)] = total

    for c in range(chunks):
        for hop in range(1, span + 1):
            line_sends(c, hop, lambda copy: copy.wait_send())
        side_copy(c).wait_send()
    for j in range(per_slab):
        for k in range(chips):
            core_copy(k, j).wait_send()
        for k in range(1, chips):
            chip_copy(k, j).wait_send()


def gather_body(n_blk, n_rep, orbitals, skew):
    n_orb, nx, ny, nz = orbitals.shape
    chunks = nx // ROWS
    levels = n_blk // COLS
    chips = n_rep // CORES
    per_slab = nx // n_rep // ROWS
    groups = ny // GROUP
    bf16, f32 = jnp.bfloat16, jnp.float32

    table_z = np.kron(np.eye(2), cas_table(nz).astype(np.float32))
    table_x = np.kron(cas_table(nx).astype(np.float32), np.eye(GROUP))
    table_y = np.einsum(
        "gky,xw->gxkwy",
        cas_table(ny).astype(np.float32).reshape(groups, GROUP, ny),
        np.eye(ROWS, dtype=np.float32),
    ).reshape(ROWS * ny, ROWS * ny)
    kernel = (
        kernel_table(nx, ny, nz)
        .reshape(nx, groups, GROUP, nz)
        .transpose(1, 0, 2, 3)
        .reshape(groups, nx * GROUP, nz)
    )
    others = HOPS // COLS
    dma = pltpu.SemaphoreType.DMA
    piece = (ROWS, ny, nz)
    scratch = (
        [pltpu.VMEM((levels, *piece), bf16) for _ in range(chunks)]
        + [pltpu.VMEM((others, *piece), bf16) for _ in range(2 * chunks)]
        + [
            pltpu.VMEM((HOPS, nx, ny, nz), bf16),
            pltpu.VMEM((HOPS * n_orb // 2, groups, nx * GROUP, 2 * nz), bf16),
            pltpu.VMEM((chips, per_slab, n_orb, *piece), bf16),
            pltpu.VMEM((chips, per_slab, n_orb, *piece), bf16),
            pltpu.VMEM((max(chips - 1, 1), per_slab, n_orb, *piece), bf16),
            pltpu.VMEM((max(chips - 1, 1), per_slab, n_orb, *piece), bf16),
            dma((chunks, max(levels - 1, 1), 2)),
            dma((chunks, max(levels - 1, 1), 2)),
            dma((chunks,)),
            dma((chunks,)),
            dma((chips, per_slab)),
            dma((chips, per_slab)),
            dma((max(chips - 1, 1), per_slab)),
            dma((max(chips - 1, 1), per_slab)),
        ]
    )
    vmem = pl.BlockSpec(memory_space=pltpu.VMEM)
    pairs = HOPS * n_orb
    return pl.pallas_call(
        functools.partial(fields_kernel, n_blk, n_rep),
        out_shape=jax.ShapeDtypeStruct((n_orb, nx // n_rep, ny, nz), f32),
        in_specs=[pl.BlockSpec(memory_space=pltpu.SMEM)] + [vmem] * 6,
        out_specs=vmem,
        scratch_shapes=scratch,
        compiler_params=pltpu.CompilerParams(
            collective_id=0, has_side_effects=True, vmem_limit_bytes=48 * 1024 * 1024
        ),
        cost_estimate=pl.CostEstimate(
            flops=4 * pairs * nx * ny * nz * (nx + ny + nz),
            bytes_accessed=2 * n_orb * nx * ny * nz,
            transcendentals=0,
        ),
    )(
        skew,
        orbitals,
        jnp.asarray(table_z, bf16),
        jnp.asarray(table_y, bf16),
        jnp.asarray(table_y.T, bf16),
        jnp.asarray(table_x, bf16),
        jnp.asarray(kernel),
    )


def solution(mesh):
    n_blk, n_rep = mesh.shape["blk"], mesh.shape["rep"]
    few = n_blk <= HOPS * COLS and n_blk % COLS == 0 and n_rep % CORES == 0
    body = functools.partial(gather_body, n_blk, n_rep) if few else shift_body
    placed = (P("blk", None, None, None), P("rep"))
    return jax.shard_map(
        body, mesh=mesh, in_specs=placed, out_specs=P("blk", "rep", None, None), check_vma=False
    )
```

```python
import functools
import math

import jax
import jax.numpy as jnp
import ml_dtypes
import numpy as np
from jax import lax
from jax.experimental import pallas as pl
from jax.experimental.pallas import tpu as pltpu
from jax.sharding import PartitionSpec as P

HOPS = 4
GROUP = 8
ROWS = 4
COLS = 2
CORES = 2
MESH = pl.DeviceIdType.MESH


def cas_table(length):
    indices = np.arange(length, dtype=np.int32)
    products = indices[:, None] * indices[None, :] % length
    angles = np.float32(2.0 * math.pi / length) * products.astype(np.float32)
    return (np.cos(angles) + np.sin(angles)).astype(ml_dtypes.bfloat16)


def frequency_squares(length):
    indices = np.arange(length, dtype=np.int32)
    signed = np.where(indices > length // 2, indices - length, indices)
    wave = np.float32(2.0 * math.pi / length) * signed.astype(np.float32)
    return wave * wave


def kernel_table(nx, ny, nz):
    squares = (
        frequency_squares(nx)[:, None, None]
        + frequency_squares(ny)[None, :, None]
        + frequency_squares(nz)[None, None, :]
    )
    safe_sq = np.where(squares > 0, squares, np.float32(1.0))
    kernel = np.where(
        squares > 0,
        np.float32(4.0 * math.pi) * -np.expm1(-squares) / safe_sq,
        np.float32(4.0 * math.pi),
    )
    return (kernel / np.float32(nx * ny * nz)).astype(np.float32)


def shifted_2(value, axis, steps):
    count = lax.axis_size(axis)
    pairs = [(source, (source + steps) % count) for source in range(count)]
    return lax.ppermute(value, axis, pairs)


def transform(field, table_x, table_y, table_z):
    first = jnp.einsum("oxyz,zk->oxyk", field, table_z, preferred_element_type=jnp.float32).astype(
        jnp.bfloat16
    )
    second = jnp.einsum("oxyz,yk->oxkz", first, table_y, preferred_element_type=jnp.float32).astype(
        jnp.bfloat16
    )
    return jnp.einsum("oxyz,xk->okyz", second, table_x, preferred_element_type=jnp.float32)


def pair_field(residents, visitor, tables, kernel):
    density = (residents.astype(jnp.float32) * visitor.astype(jnp.float32)[None]).astype(
        jnp.bfloat16
    )
    forward = transform(density, *tables).astype(jnp.bfloat16)
    scaled = (kernel[None] * forward.astype(jnp.float32)).astype(jnp.bfloat16)
    potential = transform(scaled, *tables)
    return potential * visitor.astype(jnp.float32)[None]


def shift_by(visitor, offset):
    for level in range((lax.axis_size("blk") - 1).bit_length()):
        shifted = shifted_2(visitor, "blk", 1 << level)
        visitor = jnp.where(offset // (1 << level) % 2 == 1, shifted, visitor)
    return visitor


def shift_body(orbitals, skew):
    _, nx, ny, nz = orbitals.shape
    tables = [jnp.asarray(cas_table(n)) for n in (nx, ny, nz)]
    kernel = jnp.asarray(kernel_table(nx, ny, nz))
    replica = lax.axis_index("rep")
    start_orb = lax.dynamic_index_in_dim(orbitals, replica % orbitals.shape[0], 0, keepdims=False)
    field_sum = jnp.zeros(orbitals.shape, jnp.float32)
    visitor = shift_by(start_orb, skew[0])
    for hop_index in range(HOPS):
        if hop_index > 0:
            visitor = shifted_2(visitor, "blk", 1)
        field_sum = field_sum + pair_field(orbitals, visitor, tables, kernel)
    return lax.psum_scatter(field_sum, "rep", scatter_dimension=1, tiled=True)


def fields_kernel(
    n_blk, n_rep, skew_ref, orb_hbm, tz_hbm, ty_hbm, tyt_hbm, tx_hbm, kern_hbm, out_ref, *scratch
):
    n_orb, nx, ny, nz = orb_hbm.shape
    chunks = nx // ROWS
    levels = n_blk // COLS
    chips = n_rep // CORES
    per_slab = nx // n_rep // ROWS
    groups = ny // GROUP
    rows = ROWS * ny
    sub = ROWS * GROUP
    others = HOPS // COLS
    halves = n_orb // 2
    columns = scratch[:chunks]
    staged = scratch[chunks : 2 * chunks]
    sides = scratch[2 * chunks : 3 * chunks]
    scratch = scratch[3 * chunks :]
    orb, tz_ref, ty_ref, tyt_ref, tx_ref, kern_ref, load_sem = scratch[:7]
    scratch = scratch[7:]
    vis, freq, send_core, recv_core, send_chip, recv_chip = scratch[:6]
    line_send, line_recv, side_send, side_recv, core_send, core_recv, chip_send, chip_recv = scratch[
        6:
    ]

    blk = lax.axis_index("blk")
    rep = lax.axis_index("rep")
    level, col = blk // COLS, blk % COLS
    chip, core = rep // CORES, rep % CORES
    side_blk = level * COLS + (COLS - 1 - col)
    core_rep = chip * CORES + (CORES - 1 - core)
    mine = rep % n_orb
    skew = skew_ref[0]

    def chip_rep(step):
        return (chip + step) % chips * CORES + core

    loads = [
        pltpu.make_async_copy(src, dst, load_sem.at[i])
        for i, (src, dst) in enumerate(
            [
                (orb_hbm, orb),
                (tz_hbm, tz_ref),
                (ty_hbm, ty_ref),
                (tx_hbm, tx_ref),
                (kern_hbm, kern_ref),
                (tyt_hbm, tyt_ref),
            ]
        )
    ]
    for load in loads:
        load.start()
    barrier = pltpu.get_barrier_semaphore()
    pl.semaphore_signal(barrier, inc=1, device_id=(side_blk, rep), device_id_type=MESH)
    pl.semaphore_signal(barrier, inc=1, device_id=(blk, core_rep), device_id_type=MESH)
    for step in range(1, chips):
        pl.semaphore_signal(barrier, inc=1, device_id=(blk, chip_rep(step)), device_id_type=MESH)

    @pl.when(level > 0)
    def _():
        pl.semaphore_signal(barrier, inc=1, device_id=(blk - COLS, rep), device_id_type=MESH)

    @pl.when(level < levels - 1)
    def _():
        pl.semaphore_signal(barrier, inc=1, device_id=(blk + COLS, rep), device_id_type=MESH)

    ends = (level == 0).astype(jnp.int32) + (level == levels - 1).astype(jnp.int32)
    pl.semaphore_wait(barrier, 2 + (chips - 1) + 2 - ends)

    def line_copy(c, hop, up):
        source = level - (hop - 1) if up else level + (hop - 1)
        way = 0 if up else 1
        if hop == 1:
            src = orb_hbm.at[mine, pl.ds(c * ROWS, ROWS)]
        else:
            src = columns[c].at[source]
        return pltpu.make_async_remote_copy(
            src_ref=src,
            dst_ref=columns[c].at[source],
            send_sem=line_send.at[c, hop - 1, way],
            recv_sem=line_recv.at[c, hop - 1, way],
            device_id=(blk + COLS if up else blk - COLS, rep),
            device_id_type=MESH,
        )

    def line_sends(c, hop, act):
        @pl.when((level < levels - 1) & (level >= hop - 1))
        def _():
            act(line_copy(c, hop, True))

        @pl.when((level > 0) & (level + hop - 1 <= levels - 1))
        def _():
            act(line_copy(c, hop, False))

    def line_arrivals(c, hop):
        def arrival(source, way):
            return pltpu.make_async_remote_copy(
                src_ref=columns[c].at[source],
                dst_ref=columns[c].at[source],
                send_sem=line_send.at[c, hop - 1, way],
                recv_sem=line_recv.at[c, hop - 1, way],
                device_id=(side_blk, rep),
                device_id_type=MESH,
            )

        @pl.when(level >= hop)
        def _():
            arrival(level - hop, 0).wait_recv()

        @pl.when(level + hop <= levels - 1)
        def _():
            arrival(level + hop, 1).wait_recv()

    def side_copy(c):
        return pltpu.make_async_remote_copy(
            src_ref=staged[c],
            dst_ref=sides[c],
            send_sem=side_send.at[c],
            recv_sem=side_recv.at[c],
            device_id=(side_blk, rep),
            device_id_type=MESH,
        )

    def send_side(c):
        first = (side_blk - skew - col) % COLS
        for j in range(others):
            owner = (side_blk - skew - first - COLS * j) % n_blk
            staged[c][j] = columns[c][owner // COLS]
        side_copy(c).start()

    def forward(c):
        for hop in range(HOPS):
            owner = (blk - skew - hop) % n_blk
            vis[hop, pl.ds(c * ROWS, ROWS)] = jnp.where(
                owner % COLS == col, columns[c][owner // COLS], sides[c][hop // COLS]
            )

        for hop in range(HOPS):
            visitor = vis[hop, pl.ds(c * ROWS, ROWS)].reshape(rows, nz)
            for half in range(halves):
                density = jnp.concatenate(
                    [
                        orb[2 * half + k, pl.ds(c * ROWS, ROWS)].reshape(rows, nz) * visitor
                        for k in range(2)
                    ],
                    axis=1,
                )
                first = jnp.dot(density, tz_ref[...], preferred_element_type=jnp.float32)
                second = jnp.dot(
                    ty_ref[...], first.astype(jnp.bfloat16), preferred_element_type=jnp.float32
                )
                freq[hop * halves + half, :, pl.ds(c * sub, sub)] = second.astype(
                    jnp.bfloat16
                ).reshape(groups, sub, 2 * nz)

    def middle(half):
        def unit(group, carry):
            factor = kern_ref[group]
            for hop in range(HOPS):
                index = hop * halves + half
                third = jnp.dot(
                    tx_ref[...], freq[index, group], preferred_element_type=jnp.float32
                )
                scaled = jnp.concatenate(
                    [third[:, :nz] * factor, third[:, nz:] * factor], axis=1
                ).astype(jnp.bfloat16)
                back = jnp.dot(tx_ref[...], scaled, preferred_element_type=jnp.float32)
                freq[index, group] = back.astype(jnp.bfloat16)
            return carry

        lax.fori_loop(0, groups, unit, 0)

    def backward(c, half, store):
        totals = [None, None]
        for hop in range(HOPS):
            visitor = vis[hop, pl.ds(c * ROWS, ROWS)].reshape(rows, nz).astype(jnp.float32)
            spectrum = freq[
                hop * halves + half, :, pl.ds(pl.multiple_of(c * sub, sub), sub)
            ].reshape(groups * sub, 2 * nz)
            first = jnp.dot(tyt_ref[...], spectrum, preferred_element_type=jnp.float32)
            potential = jnp.dot(
                first.astype(jnp.bfloat16), tz_ref[...], preferred_element_type=jnp.float32
            )
            for k in range(2):
                term = potential[:, k * nz : (k + 1) * nz] * visitor
                totals[k] = term if hop == 0 else totals[k] + term
        for k in range(2):
            store(2 * half + k, totals[k].reshape(ROWS, ny, nz))

    span = levels - 1
    ahead = 2
    for c in range(ahead):
        line_sends(c, 1, lambda copy: copy.start())
    for load in loads:
        load.wait()
    for c in range(chunks):
        columns[c][level] = orb[mine, pl.ds(c * ROWS, ROWS)]
    for step in range(chunks + span + 1):
        if step + ahead < chunks:
            line_sends(step + ahead, 1, lambda copy: copy.start())
        for hop in range(2, span + 1):
            c = step - (hop - 1)
            if 0 <= c < chunks:
                line_arrivals(c, hop - 1)
                line_sends(c, hop, lambda copy: copy.start())
        c = step - span
        if 0 <= c < chunks:
            line_arrivals(c, span)
            send_side(c)
        c = step - span - 1
        if 0 <= c < chunks:
            side_copy(c).wait_recv()
            forward(c)

    def core_copy(k, j, half):
        both = pl.ds(2 * half, 2)
        return pltpu.make_async_remote_copy(
            src_ref=send_core.at[k, j, both],
            dst_ref=recv_core.at[k, j, both],
            send_sem=core_send.at[k, j, half],
            recv_sem=core_recv.at[k, j, half],
            device_id=(blk, core_rep),
            device_id_type=MESH,
        )

    def chip_copy(k, j, half):
        both = pl.ds(2 * half, 2)
        return pltpu.make_async_remote_copy(
            src_ref=send_chip.at[k - 1, j, both],
            dst_ref=recv_chip.at[k - 1, j, both],
            send_sem=chip_send.at[k - 1, j, half],
            recv_sem=chip_recv.at[k - 1, j, half],
            device_id=(blk, chip_rep(k)),
            device_id_type=MESH,
        )

    def finish(half):
        for j in range(per_slab):
            core_copy(0, j, half).wait_recv()
            for k in range(1, chips):
                chip_copy(k, j, half).wait_recv()
            for orbital in range(2 * half, 2 * half + 2):
                total = out_ref[orbital, pl.ds(j * ROWS, ROWS)]
                total = total + recv_core[0, j, orbital].astype(jnp.float32)
                for k in range(1, chips):
                    total = total + recv_chip[k - 1, j, orbital].astype(jnp.float32)
                out_ref[orbital, pl.ds(j * ROWS, ROWS)] = total

    for half in range(halves):
        middle(half)
        for k in list(range(1, chips)) + [0]:
            home = (chip + k) % chips * CORES
            for j in range(per_slab):

                def store_core(orbital, value):
                    send_core[k, j, orbital] = value.astype(jnp.bfloat16)

                backward((home + CORES - 1 - core) * per_slab + j, half, store_core)
                core_copy(k, j, half).start()
            for j in range(per_slab if k > 0 else 0):

                def store_partial(orbital, value):
                    out_ref[orbital, pl.ds(j * ROWS, ROWS)] = value

                backward((home + core) * per_slab + j, half, store_partial)
                core_copy(k, j, half).wait_recv()
                for orbital in range(2 * half, 2 * half + 2):
                    send_chip[k - 1, j, orbital] = (
                        out_ref[orbital, pl.ds(j * ROWS, ROWS)]
                        + recv_core[k, j, orbital].astype(jnp.float32)
                    ).astype(jnp.bfloat16)
                chip_copy(k, j, half).start()
        for j in range(per_slab):

            def store_out(orbital, value):
                out_ref[orbital, pl.ds(j * ROWS, ROWS)] = value

            backward(rep * per_slab + j, half, store_out)
    for half in range(halves):
        finish(half)

    for c in range(chunks):
        for hop in range(1, span + 1):
            line_sends(c, hop, lambda copy: copy.wait_send())
        side_copy(c).wait_send()
    for half in range(halves):
        for j in range(per_slab):
            for k in range(chips):
                core_copy(k, j, half).wait_send()
            for k in range(1, chips):
                chip_copy(k, j, half).wait_send()


def gather_body(n_blk, n_rep, orbitals, skew):
    n_orb, nx, ny, nz = orbitals.shape
    chunks = nx // ROWS
    levels = n_blk // COLS
    chips = n_rep // CORES
    per_slab = nx // n_rep // ROWS
    groups = ny // GROUP
    bf16, f32 = jnp.bfloat16, jnp.float32

    table_z = np.kron(np.eye(2), cas_table(nz).astype(np.float32))
    table_x = np.kron(cas_table(nx).astype(np.float32), np.eye(GROUP))
    table_y = np.einsum(
        "gky,xw->gxkwy",
        cas_table(ny).astype(np.float32).reshape(groups, GROUP, ny),
        np.eye(ROWS, dtype=np.float32),
    ).reshape(ROWS * ny, ROWS * ny)
    kernel = (
        kernel_table(nx, ny, nz)
        .reshape(nx, groups, GROUP, nz)
        .transpose(1, 0, 2, 3)
        .reshape(groups, nx * GROUP, nz)
    )
    others = HOPS // COLS
    dma = pltpu.SemaphoreType.DMA
    piece = (ROWS, ny, nz)
    scratch = (
        [pltpu.VMEM((levels, *piece), bf16) for _ in range(chunks)]
        + [pltpu.VMEM((others, *piece), bf16) for _ in range(2 * chunks)]
        + [
            pltpu.VMEM((n_orb, nx, ny, nz), bf16),
            pltpu.VMEM(table_z.shape, bf16),
            pltpu.VMEM(table_y.shape, bf16),
            pltpu.VMEM(table_y.shape, bf16),
            pltpu.VMEM(table_x.shape, bf16),
            pltpu.VMEM(kernel.shape, f32),
            dma((6,)),
            pltpu.VMEM((HOPS, nx, ny, nz), bf16),
            pltpu.VMEM((HOPS * n_orb // 2, groups, nx * GROUP, 2 * nz), bf16),
            pltpu.VMEM((chips, per_slab, n_orb, *piece), bf16),
            pltpu.VMEM((chips, per_slab, n_orb, *piece), bf16),
            pltpu.VMEM((max(chips - 1, 1), per_slab, n_orb, *piece), bf16),
            pltpu.VMEM((max(chips - 1, 1), per_slab, n_orb, *piece), bf16),
            dma((chunks, max(levels - 1, 1), 2)),
            dma((chunks, max(levels - 1, 1), 2)),
            dma((chunks,)),
            dma((chunks,)),
            dma((chips, per_slab, n_orb // 2)),
            dma((chips, per_slab, n_orb // 2)),
            dma((max(chips - 1, 1), per_slab, n_orb // 2)),
            dma((max(chips - 1, 1), per_slab, n_orb // 2)),
        ]
    )
    vmem = pl.BlockSpec(memory_space=pltpu.VMEM)
    pairs = HOPS * n_orb
    return pl.pallas_call(
        functools.partial(fields_kernel, n_blk, n_rep),
        out_shape=jax.ShapeDtypeStruct((n_orb, nx // n_rep, ny, nz), f32),
        in_specs=[pl.BlockSpec(memory_space=pltpu.SMEM)]
        + [pl.BlockSpec(memory_space=pltpu.HBM)] * 6,
        out_specs=vmem,
        scratch_shapes=scratch,
        compiler_params=pltpu.CompilerParams(
            collective_id=0, has_side_effects=True, vmem_limit_bytes=48 * 1024 * 1024
        ),
        cost_estimate=pl.CostEstimate(
            flops=4 * pairs * nx * ny * nz * (nx + ny + nz),
            bytes_accessed=2 * n_orb * nx * ny * nz,
            transcendentals=0,
        ),
    )(
        skew,
        orbitals,
        jnp.asarray(table_z, bf16),
        jnp.asarray(table_y, bf16),
        jnp.asarray(table_y.T, bf16),
        jnp.asarray(table_x, bf16),
        jnp.asarray(kernel),
    )


def solution(mesh):
    n_blk, n_rep = mesh.shape["blk"], mesh.shape["rep"]
    few = n_blk <= HOPS * COLS and n_blk % COLS == 0 and n_rep % CORES == 0
    body = functools.partial(gather_body, n_blk, n_rep) if few else shift_body
    placed = (P("blk", None, None, None), P("rep"))
    return jax.shard_map(
        body, mesh=mesh, in_specs=placed, out_specs=P("blk", "rep", None, None), check_vma=False
    )
```

```python
import functools
import math

import jax
import jax.numpy as jnp
import ml_dtypes
import numpy as np
from jax import lax
from jax.experimental import pallas as pl
from jax.experimental.pallas import tpu as pltpu
from jax.sharding import PartitionSpec as P

HOPS = 4
GROUP = 8
ROWS = 4
COLS = 2
CORES = 2
MESH = pl.DeviceIdType.MESH


def cas_table(length):
    indices = np.arange(length, dtype=np.int32)
    products = indices[:, None] * indices[None, :] % length
    angles = np.float32(2.0 * math.pi / length) * products.astype(np.float32)
    return (np.cos(angles) + np.sin(angles)).astype(ml_dtypes.bfloat16)


def frequency_squares(length):
    indices = np.arange(length, dtype=np.int32)
    signed = np.where(indices > length // 2, indices - length, indices)
    wave = np.float32(2.0 * math.pi / length) * signed.astype(np.float32)
    return wave * wave


def kernel_table(nx, ny, nz):
    squares = (
        frequency_squares(nx)[:, None, None]
        + frequency_squares(ny)[None, :, None]
        + frequency_squares(nz)[None, None, :]
    )
    safe_sq = np.where(squares > 0, squares, np.float32(1.0))
    kernel = np.where(
        squares > 0,
        np.float32(4.0 * math.pi) * -np.expm1(-squares) / safe_sq,
        np.float32(4.0 * math.pi),
    )
    return (kernel / np.float32(nx * ny * nz)).astype(np.float32)


def shifted_2(value, axis, steps):
    count = lax.axis_size(axis)
    pairs = [(source, (source + steps) % count) for source in range(count)]
    return lax.ppermute(value, axis, pairs)


def transform(field, table_x, table_y, table_z):
    first = jnp.einsum("oxyz,zk->oxyk", field, table_z, preferred_element_type=jnp.float32).astype(
        jnp.bfloat16
    )
    second = jnp.einsum("oxyz,yk->oxkz", first, table_y, preferred_element_type=jnp.float32).astype(
        jnp.bfloat16
    )
    return jnp.einsum("oxyz,xk->okyz", second, table_x, preferred_element_type=jnp.float32)


def pair_field(residents, visitor, tables, kernel):
    density = (residents.astype(jnp.float32) * visitor.astype(jnp.float32)[None]).astype(
        jnp.bfloat16
    )
    forward = transform(density, *tables).astype(jnp.bfloat16)
    scaled = (kernel[None] * forward.astype(jnp.float32)).astype(jnp.bfloat16)
    potential = transform(scaled, *tables)
    return potential * visitor.astype(jnp.float32)[None]


def shift_by(visitor, offset):
    for level in range((lax.axis_size("blk") - 1).bit_length()):
        shifted = shifted_2(visitor, "blk", 1 << level)
        visitor = jnp.where(offset // (1 << level) % 2 == 1, shifted, visitor)
    return visitor


def shift_body(orbitals, skew):
    _, nx, ny, nz = orbitals.shape
    tables = [jnp.asarray(cas_table(n)) for n in (nx, ny, nz)]
    kernel = jnp.asarray(kernel_table(nx, ny, nz))
    replica = lax.axis_index("rep")
    start_orb = lax.dynamic_index_in_dim(orbitals, replica % orbitals.shape[0], 0, keepdims=False)
    field_sum = jnp.zeros(orbitals.shape, jnp.float32)
    visitor = shift_by(start_orb, skew[0])
    for hop_index in range(HOPS):
        if hop_index > 0:
            visitor = shifted_2(visitor, "blk", 1)
        field_sum = field_sum + pair_field(orbitals, visitor, tables, kernel)
    return lax.psum_scatter(field_sum, "rep", scatter_dimension=1, tiled=True)


def fields_kernel(
    n_blk, n_rep, skew_ref, orb_hbm, tz_hbm, ty_hbm, tyt_hbm, tx_hbm, kern_hbm, out_ref, *scratch
):
    n_orb, nx, ny, nz = orb_hbm.shape
    chunks = nx // ROWS
    levels = n_blk // COLS
    chips = n_rep // CORES
    per_slab = nx // n_rep // ROWS
    groups = ny // GROUP
    rows = ROWS * ny
    sub = ROWS * GROUP
    others = HOPS // COLS
    halves = n_orb // 2
    columns = scratch[:chunks]
    staged = scratch[chunks : 2 * chunks]
    sides = scratch[2 * chunks : 3 * chunks]
    scratch = scratch[3 * chunks :]
    orb, tz_ref, ty_ref, tyt_ref, tx_ref, kern_ref, load_sem = scratch[:7]
    scratch = scratch[7:]
    vis, freq, send_core, recv_core, send_chip, recv_chip = scratch[:6]
    line_send, line_recv, side_send, side_recv, core_send, core_recv, chip_send, chip_recv = scratch[
        6:
    ]

    blk = lax.axis_index("blk")
    rep = lax.axis_index("rep")
    level, col = blk // COLS, blk % COLS
    chip, core = rep // CORES, rep % CORES
    side_blk = level * COLS + (COLS - 1 - col)
    core_rep = chip * CORES + (CORES - 1 - core)
    mine = rep % n_orb
    skew = skew_ref[0]

    def chip_rep(step):
        return (chip + step) % chips * CORES + core

    loads = [
        pltpu.make_async_copy(src, dst, load_sem.at[i])
        for i, (src, dst) in enumerate(
            [
                (orb_hbm, orb),
                (tz_hbm, tz_ref),
                (ty_hbm, ty_ref),
                (tx_hbm, tx_ref),
                (kern_hbm, kern_ref),
                (tyt_hbm, tyt_ref),
            ]
        )
    ]
    for load in loads:
        load.start()
    barrier = pltpu.get_barrier_semaphore()
    pl.semaphore_signal(barrier, inc=1, device_id=(side_blk, rep), device_id_type=MESH)
    pl.semaphore_signal(barrier, inc=1, device_id=(blk, core_rep), device_id_type=MESH)
    for step in range(1, chips):
        pl.semaphore_signal(barrier, inc=1, device_id=(blk, chip_rep(step)), device_id_type=MESH)

    @pl.when(level > 0)
    def _():
        pl.semaphore_signal(barrier, inc=1, device_id=(blk - COLS, rep), device_id_type=MESH)

    @pl.when(level < levels - 1)
    def _():
        pl.semaphore_signal(barrier, inc=1, device_id=(blk + COLS, rep), device_id_type=MESH)

    ends = (level == 0).astype(jnp.int32) + (level == levels - 1).astype(jnp.int32)
    pl.semaphore_wait(barrier, 2 + (chips - 1) + 2 - ends)

    def line_copy(c, hop, up):
        source = level - (hop - 1) if up else level + (hop - 1)
        way = 0 if up else 1
        if hop == 1:
            src = orb_hbm.at[mine, pl.ds(c * ROWS, ROWS)]
        else:
            src = columns[c].at[source]
        return pltpu.make_async_remote_copy(
            src_ref=src,
            dst_ref=columns[c].at[source],
            send_sem=line_send.at[c, hop - 1, way],
            recv_sem=line_recv.at[c, hop - 1, way],
            device_id=(blk + COLS if up else blk - COLS, rep),
            device_id_type=MESH,
        )

    def line_sends(c, hop, act):
        @pl.when((level < levels - 1) & (level >= hop - 1))
        def _():
            act(line_copy(c, hop, True))

        @pl.when((level > 0) & (level + hop - 1 <= levels - 1))
        def _():
            act(line_copy(c, hop, False))

    def line_arrivals(c, hop):
        def arrival(source, way):
            return pltpu.make_async_remote_copy(
                src_ref=columns[c].at[source],
                dst_ref=columns[c].at[source],
                send_sem=line_send.at[c, hop - 1, way],
                recv_sem=line_recv.at[c, hop - 1, way],
                device_id=(side_blk, rep),
                device_id_type=MESH,
            )

        @pl.when(level >= hop)
        def _():
            arrival(level - hop, 0).wait_recv()

        @pl.when(level + hop <= levels - 1)
        def _():
            arrival(level + hop, 1).wait_recv()

    def side_copy(c):
        return pltpu.make_async_remote_copy(
            src_ref=staged[c],
            dst_ref=sides[c],
            send_sem=side_send.at[c],
            recv_sem=side_recv.at[c],
            device_id=(side_blk, rep),
            device_id_type=MESH,
        )

    def send_side(c):
        first = (side_blk - skew - col) % COLS
        for j in range(others):
            owner = (side_blk - skew - first - COLS * j) % n_blk
            staged[c][j] = columns[c][owner // COLS]
        side_copy(c).start()

    def forward(c):
        for hop in range(HOPS):
            owner = (blk - skew - hop) % n_blk
            vis[hop, pl.ds(c * ROWS, ROWS)] = jnp.where(
                owner % COLS == col, columns[c][owner // COLS], sides[c][hop // COLS]
            )

        for hop in range(HOPS):
            visitor = vis[hop, pl.ds(c * ROWS, ROWS)].reshape(rows, nz)
            for half in range(halves):
                density = jnp.concatenate(
                    [
                        orb[2 * half + k, pl.ds(c * ROWS, ROWS)].reshape(rows, nz) * visitor
                        for k in range(2)
                    ],
                    axis=1,
                )
                first = jnp.dot(density, tz_ref[...], preferred_element_type=jnp.float32)
                second = jnp.dot(
                    ty_ref[...], first.astype(jnp.bfloat16), preferred_element_type=jnp.float32
                )
                freq[hop * halves + half, :, pl.ds(c * sub, sub)] = second.astype(
                    jnp.bfloat16
                ).reshape(groups, sub, 2 * nz)

    def middle(half):
        def unit(group, carry):
            factor = kern_ref[group]
            for hop in range(HOPS):
                index = hop * halves + half
                third = jnp.dot(
                    tx_ref[...], freq[index, group], preferred_element_type=jnp.float32
                )
                scaled = jnp.concatenate(
                    [third[:, :nz] * factor, third[:, nz:] * factor], axis=1
                ).astype(jnp.bfloat16)
                back = jnp.dot(tx_ref[...], scaled, preferred_element_type=jnp.float32)
                freq[index, group] = back.astype(jnp.bfloat16)
            return carry

        lax.fori_loop(0, groups, unit, 0)

    def backward(c, half, store):
        totals = [None, None]
        for hop in range(HOPS):
            visitor = vis[hop, pl.ds(c * ROWS, ROWS)].reshape(rows, nz).astype(jnp.float32)
            spectrum = freq[
                hop * halves + half, :, pl.ds(pl.multiple_of(c * sub, sub), sub)
            ].reshape(groups * sub, 2 * nz)
            first = jnp.dot(tyt_ref[...], spectrum, preferred_element_type=jnp.float32)
            potential = jnp.dot(
                first.astype(jnp.bfloat16), tz_ref[...], preferred_element_type=jnp.float32
            )
            for k in range(2):
                term = potential[:, k * nz : (k + 1) * nz] * visitor
                totals[k] = term if hop == 0 else totals[k] + term
        for k in range(2):
            store(2 * half + k, totals[k].reshape(ROWS, ny, nz))

    span = levels - 1
    ahead = 2
    for c in range(ahead):
        line_sends(c, 1, lambda copy: copy.start())
    for load in loads:
        load.wait()
    for c in range(chunks):
        columns[c][level] = orb[mine, pl.ds(c * ROWS, ROWS)]
    for step in range(chunks + span + 1):
        if step + ahead < chunks:
            line_sends(step + ahead, 1, lambda copy: copy.start())
        for hop in range(2, span + 1):
            c = step - (hop - 1)
            if 0 <= c < chunks:
                line_arrivals(c, hop - 1)
                line_sends(c, hop, lambda copy: copy.start())
        c = step - span
        if 0 <= c < chunks:
            line_arrivals(c, span)
            send_side(c)
        c = step - span - 1
        if 0 <= c < chunks:
            side_copy(c).wait_recv()
            forward(c)

    def core_copy(k, j, half):
        both = pl.ds(2 * half, 2)
        return pltpu.make_async_remote_copy(
            src_ref=send_core.at[k, j, both],
            dst_ref=recv_core.at[k, j, both],
            send_sem=core_send.at[k, j, half],
            recv_sem=core_recv.at[k, j, half],
            device_id=(blk, core_rep),
            device_id_type=MESH,
        )

    def chip_copy(k, j, half):
        both = pl.ds(2 * half, 2)
        return pltpu.make_async_remote_copy(
            src_ref=send_chip.at[k - 1, j, both],
            dst_ref=recv_chip.at[k - 1, j, both],
            send_sem=chip_send.at[k - 1, j, half],
            recv_sem=chip_recv.at[k - 1, j, half],
            device_id=(blk, chip_rep(k)),
            device_id_type=MESH,
        )

    def finish(half):
        for j in range(per_slab):
            core_copy(0, j, half).wait_recv()
            for k in range(1, chips):
                chip_copy(k, j, half).wait_recv()
            for orbital in range(2 * half, 2 * half + 2):
                total = out_ref[orbital, pl.ds(j * ROWS, ROWS)]
                total = total + recv_core[0, j, orbital].astype(jnp.float32)
                for k in range(1, chips):
                    total = total + recv_chip[k - 1, j, orbital].astype(jnp.float32)
                out_ref[orbital, pl.ds(j * ROWS, ROWS)] = total

    for half in range(halves):
        middle(half)
        for k in list(range(1, chips)) + [0]:
            home = (chip + k) % chips * CORES
            for j in range(per_slab):

                def store_core(orbital, value):
                    send_core[k, j, orbital] = value.astype(jnp.bfloat16)

                backward((home + CORES - 1 - core) * per_slab + j, half, store_core)
                core_copy(k, j, half).start()
            for j in range(per_slab if k > 0 else 0):

                def store_partial(orbital, value):
                    out_ref[orbital, pl.ds(j * ROWS, ROWS)] = value

                backward((home + core) * per_slab + j, half, store_partial)
                core_copy(k, j, half).wait_recv()
                for orbital in range(2 * half, 2 * half + 2):
                    send_chip[k - 1, j, orbital] = (
                        out_ref[orbital, pl.ds(j * ROWS, ROWS)]
                        + recv_core[k, j, orbital].astype(jnp.float32)
                    ).astype(jnp.bfloat16)
                chip_copy(k, j, half).start()
        for j in range(per_slab):

            def store_out(orbital, value):
                out_ref[orbital, pl.ds(j * ROWS, ROWS)] = value

            backward(rep * per_slab + j, half, store_out)
    for half in range(halves):
        finish(half)

    for c in range(chunks):
        for hop in range(1, span + 1):
            line_sends(c, hop, lambda copy: copy.wait_send())
        side_copy(c).wait_send()
    for half in range(halves):
        for j in range(per_slab):
            for k in range(chips):
                core_copy(k, j, half).wait_send()
            for k in range(1, chips):
                chip_copy(k, j, half).wait_send()


def gather_body(n_blk, n_rep, orbitals, skew):
    n_orb, nx, ny, nz = orbitals.shape
    chunks = nx // ROWS
    levels = n_blk // COLS
    chips = n_rep // CORES
    per_slab = nx // n_rep // ROWS
    groups = ny // GROUP
    bf16, f32 = jnp.bfloat16, jnp.float32

    table_z = np.kron(np.eye(2), cas_table(nz).astype(np.float32))
    table_x = np.kron(cas_table(nx).astype(np.float32), np.eye(GROUP))
    table_y = np.einsum(
        "gky,xw->gxkwy",
        cas_table(ny).astype(np.float32).reshape(groups, GROUP, ny),
        np.eye(ROWS, dtype=np.float32),
    ).reshape(ROWS * ny, ROWS * ny)
    kernel = (
        kernel_table(nx, ny, nz)
        .reshape(nx, groups, GROUP, nz)
        .transpose(1, 0, 2, 3)
        .reshape(groups, nx * GROUP, nz)
    )
    others = HOPS // COLS
    dma = pltpu.SemaphoreType.DMA
    piece = (ROWS, ny, nz)
    scratch = (
        [pltpu.VMEM((levels, *piece), bf16) for _ in range(chunks)]
        + [pltpu.VMEM((others, *piece), bf16) for _ in range(2 * chunks)]
        + [
            pltpu.VMEM((n_orb, nx, ny, nz), bf16),
            pltpu.VMEM(table_z.shape, bf16),
            pltpu.VMEM(table_y.shape, bf16),
            pltpu.VMEM(table_y.shape, bf16),
            pltpu.VMEM(table_x.shape, bf16),
            pltpu.VMEM(kernel.shape, f32),
            dma((6,)),
            pltpu.VMEM((HOPS, nx, ny, nz), bf16),
            pltpu.VMEM((HOPS * n_orb // 2, groups, nx * GROUP, 2 * nz), bf16),
            pltpu.VMEM((chips, per_slab, n_orb, *piece), bf16),
            pltpu.VMEM((chips, per_slab, n_orb, *piece), bf16),
            pltpu.VMEM((max(chips - 1, 1), per_slab, n_orb, *piece), bf16),
            pltpu.VMEM((max(chips - 1, 1), per_slab, n_orb, *piece), bf16),
            dma((chunks, max(levels - 1, 1), 2)),
            dma((chunks, max(levels - 1, 1), 2)),
            dma((chunks,)),
            dma((chunks,)),
            dma((chips, per_slab, n_orb // 2)),
            dma((chips, per_slab, n_orb // 2)),
            dma((max(chips - 1, 1), per_slab, n_orb // 2)),
            dma((max(chips - 1, 1), per_slab, n_orb // 2)),
        ]
    )
    vmem = pl.BlockSpec(memory_space=pltpu.VMEM)
    pairs = HOPS * n_orb
    return pl.pallas_call(
        functools.partial(fields_kernel, n_blk, n_rep),
        out_shape=jax.ShapeDtypeStruct((n_orb, nx // n_rep, ny, nz), f32),
        in_specs=[pl.BlockSpec(memory_space=pltpu.SMEM)]
        + [pl.BlockSpec(memory_space=pltpu.HBM)] * 6,
        out_specs=vmem,
        scratch_shapes=scratch,
        compiler_params=pltpu.CompilerParams(
            collective_id=0, has_side_effects=True, vmem_limit_bytes=64 * 1024 * 1024 - 64 * 1024
        ),
        cost_estimate=pl.CostEstimate(
            flops=4 * pairs * nx * ny * nz * (nx + ny + nz),
            bytes_accessed=2 * n_orb * nx * ny * nz,
            transcendentals=0,
        ),
    )(
        skew,
        orbitals,
        jnp.asarray(table_z, bf16),
        jnp.asarray(table_y, bf16),
        jnp.asarray(table_y.T, bf16),
        jnp.asarray(table_x, bf16),
        jnp.asarray(kernel),
    )


def solution(mesh):
    n_blk, n_rep = mesh.shape["blk"], mesh.shape["rep"]
    few = n_blk <= HOPS * COLS and n_blk % COLS == 0 and n_rep % CORES == 0
    body = functools.partial(gather_body, n_blk, n_rep) if few else shift_body
    placed = (P("blk", None, None, None), P("rep"))
    return jax.shard_map(
        body, mesh=mesh, in_specs=placed, out_specs=P("blk", "rep", None, None), check_vma=False
    )
```
